256 devices in a mesh: seq: 32 (over x, z), head: 8 (over y, core).
Axes of the slice: x: 4, y: 4, z: 8, core: 2. Of those that a mesh axis runs over, the one named last changes fastest.
Arguments:
- query_rows: bfloat16 [32768, 5120], P(('seq', 'head')), may hold values from -16 to 16
- key_rows: bfloat16 [32768, 5120], P(('seq', 'head')), may hold values from -16 to 16
- value_rows: bfloat16 [32768, 5120], P(('seq', 'head')), may hold values from -6 to 6
- head_kind: int32 [40], replicated, may hold values from 0 to 1, as said below
- frame_window: int32 [40], replicated, may hold values from 0 to 1, as said below
Outputs:
- attended: bfloat16 [32768, 5120], P(('seq', 'head'))
The draws below stay inside these ranges and needn't reach their ends.
Inputs may be any that keep to these rules, and one draw needn't show every extreme that they name: `head_kind`: some head is spatial and some head is temporal. `frame_window`: some head has window 1.
All inputs are finite; a program needn't handle non-finite values.
Results may differ from the reference program's by a relative error of at most 0.004.
Values may be sent and summed in bfloat16 or wider, within the bound.
No kernel may reach another device: no remote copies, remote signals or barrier semaphores. Data moves between devices by JAX's collectives and lax.ppermute only.
A program may use at most 64 MiB of HBM per device.

```python
import jax
import jax.numpy as jnp
from jax import lax

HEADS = 40
HEAD_DIM = 128
MAXW = 1
POS = 1024
FRAMES = 32
TOKENS = 32768


def draw_query_rows(key, part):
    own_key = jax.random.fold_in(key, 1)
    rows = jnp.clip(jax.random.normal(own_key, (TOKENS, HEADS * HEAD_DIM), jnp.float32), -6.0, 6.0)
    return rows.astype(jnp.bfloat16)


def draw_key_rows(key, part):
    own_key = jax.random.fold_in(key, 2)
    rows = jnp.clip(jax.random.normal(own_key, (TOKENS, HEADS * HEAD_DIM), jnp.float32), -6.0, 6.0)
    return rows.astype(jnp.bfloat16)


def draw_head_kind(key, part):
    key = jax.random.fold_in(key, 5)
    kinds = jax.random.randint(jax.random.fold_in(key, 1), (HEADS,), 0, 2)
    first = jax.random.randint(jax.random.fold_in(key, 2), (), 0, HEADS)
    second = (first + 1 + jax.random.randint(jax.random.fold_in(key, 3), (), 0, HEADS - 1)) % HEADS
    kinds = kinds.at[first].set(0).at[second].set(1)
    return kinds.astype(jnp.int32)


def draw_frame_window(key, part):
    key = jax.random.fold_in(key, 6)
    windows = jax.random.randint(jax.random.fold_in(key, 1), (HEADS,), 0, MAXW + 1)
    chosen = jax.random.randint(jax.random.fold_in(key, 2), (), 0, HEADS)
    windows = windows.at[chosen].set(MAXW)
    return windows.astype(jnp.int32)


def block_scale(key, dims, split, smallest, top_value):
    loudness = 1.0
    for dim, blocks in split:
        heights = jax.random.uniform(jax.random.fold_in(jax.random.fold_in(key, 6), dim), (blocks,), jnp.float32, smallest / len(split), top_value / len(split))
        loudness = loudness * jnp.repeat(jnp.exp(heights), dims[dim] // blocks).reshape((-1,) + (1,) * (len(dims) - 1 - dim))
    return loudness


def gaussian(stream_key, shape, width, bound, cuts=(), kind=jnp.bfloat16):
    level = block_scale(stream_key, shape, cuts, -0.22, 0.18) if cuts else 1.0
    drawn = jax.random.normal(stream_key, shape, jnp.float32) * width * level
    return jnp.minimum(jnp.maximum(drawn, -bound), bound).astype(kind)


def setup_inputs(seed: int = 0) -> dict:
    streams_of = jax.random.split(jax.random.key(seed), 6)
    query_rows = draw_query_rows(jax.random.fold_in(streams_of[5], 71), 0)
    key_rows = draw_key_rows(jax.random.fold_in(streams_of[5], 71), 0)
    value_rows = gaussian(streams_of[2], (TOKENS, HEADS * HEAD_DIM), 1.0, 6.0, ((0, 256),))
    head_kind = draw_head_kind(jax.random.fold_in(streams_of[5], 71), 0)
    frame_window = draw_frame_window(jax.random.fold_in(streams_of[5], 71), 0)
    return dict(query_rows=query_rows, key_rows=key_rows, value_rows=value_rows, head_kind=head_kind, frame_window=frame_window)


def spatial_head(queries, keys_all, values_all, reach):
    padding = jnp.zeros((MAXW, POS, HEAD_DIM), jnp.bfloat16)
    keys_padded = jnp.concatenate([padding, keys_all, padding], axis=0)
    values_padded = jnp.concatenate([padding, values_all, padding], axis=0)
    offsets = jnp.arange(2 * MAXW + 1, dtype=jnp.int32) - MAXW
    factor = HEAD_DIM ** -0.5

    def frame_out(frame):
        keys_near = lax.dynamic_slice_in_dim(keys_padded, frame, 2 * MAXW + 1, 0).reshape(-1, HEAD_DIM)
        values_near = lax.dynamic_slice_in_dim(values_padded, frame, 2 * MAXW + 1, 0).reshape(-1, HEAD_DIM)
        usable = (jnp.abs(offsets) <= reach) & (frame + offsets >= 0) & (frame + offsets < FRAMES)
        allowed = jnp.repeat(usable, POS)
        query_frame = lax.dynamic_index_in_dim(queries, frame, 0, keepdims=False)
        scores = lax.dot_general(query_frame, keys_near, (((1,), (1,)), ((), ())), preferred_element_type=jnp.float32) * factor
        scores = jnp.where(allowed[None, :], scores, jnp.float32(-1e30))
        top = jnp.max(scores, axis=1, keepdims=True)
        weights = jnp.where(allowed[None, :], jnp.exp(scores - top), jnp.float32(0.0))
        total = jnp.sum(weights, axis=1, keepdims=True)
        mixed = jnp.dot(weights.astype(jnp.bfloat16), values_near, preferred_element_type=jnp.float32) / total
        return mixed.astype(jnp.bfloat16)

    return lax.map(frame_out, jnp.arange(FRAMES, dtype=jnp.int32))


def temporal_head(queries, keys_all, values_all):
    factor = HEAD_DIM ** -0.5
    scores = jnp.einsum("fpd,gpd->pfg", queries.astype(jnp.float32), keys_all.astype(jnp.float32)) * factor
    top = jnp.max(scores, axis=2, keepdims=True)
    weights = jnp.exp(scores - top)
    total = jnp.sum(weights, axis=2, keepdims=True)
    rounded = weights.astype(jnp.bfloat16).astype(jnp.float32)
    mixed = jnp.einsum("pfg,gpd->fpd", rounded, values_all.astype(jnp.float32))
    return (mixed / total.transpose(1, 0, 2)).astype(jnp.bfloat16)


def reference(query_rows, key_rows, value_rows, head_kind, frame_window):
    query_grid = query_rows.reshape(FRAMES, POS, HEADS, HEAD_DIM)
    key_grid = key_rows.reshape(FRAMES, POS, HEADS, HEAD_DIM)
    value_grid = value_rows.reshape(FRAMES, POS, HEADS, HEAD_DIM)

    def head_out(head):
        queries = lax.dynamic_index_in_dim(query_grid, head, 2, keepdims=False)
        keys_all = lax.dynamic_index_in_dim(key_grid, head, 2, keepdims=False)
        values_all = lax.dynamic_index_in_dim(value_grid, head, 2, keepdims=False)
        return lax.cond(head_kind[head] == 0,
                        lambda: spatial_head(queries, keys_all, values_all, frame_window[head]),
                        lambda: temporal_head(queries, keys_all, values_all))

    outputs = lax.map(head_out, jnp.arange(HEADS, dtype=jnp.int32))
    return outputs.transpose(1, 2, 0, 3).reshape(TOKENS, HEADS * HEAD_DIM)
```

```python
import functools

import jax
import jax.numpy as jnp
from jax import lax
from jax.experimental import pallas as pl
from jax.experimental.pallas import tpu as pltpu
from jax.sharding import PartitionSpec as P

BF16 = jnp.bfloat16
F32 = jnp.float32
LOG2E = 1.4426950408889634
SMEM = pl.BlockSpec(memory_space=pltpu.SMEM)
HBM = pl.BlockSpec(memory_space=pltpu.HBM)
ANY = pl.BlockSpec(memory_space=pl.ANY)
VMEM = pl.BlockSpec(memory_space=pltpu.VMEM)
MIB = 1024 * 1024
TILE = 16

VARIANTS = (
    (4, 7, 4),
    (5, 6, 2),
    (5, 6, 3),
    (5, 6, 4),
    (6, 5, 2),
    (6, 5, 3),
    (7, 4, 4),
    (10, 10, 10),
)


def in_hbm(value):
    return pltpu.with_memory_space_constraint(value, pltpu.HBM)


def params(vmem=1):
    return pltpu.CompilerParams(vmem_limit_bytes=vmem * MIB)


def cost(flops, bytes_accessed):
    return pl.CostEstimate(flops=flops, bytes_accessed=bytes_accessed, transcendentals=0)


def chip_here():
    return lax.div(lax.axis_index("head"), jnp.int32(2))


def head_loop(kind_ref, win_ref, wide, on_temporal, on_spatial):
    total = kind_ref.shape[0]

    def body(h, counts):
        seen_t, seen_w, seen_n = counts
        is_t = kind_ref[h]
        is_w = (1 - is_t) * win_ref[h]
        is_n = (1 - is_t) * (1 - win_ref[h])
        if on_temporal is not None:
            pl.when(is_t == 1)(lambda: on_temporal(h, seen_t))
        if on_spatial is not None:
            rank = jnp.where(is_w == 1, seen_w, wide + seen_n)
            pl.when(is_t == 0)(lambda: on_spatial(h, rank))
        return seen_t + is_t, seen_w + is_w, seen_n + is_n

    zero = jnp.int32(0)
    return lax.fori_loop(0, total, body, (zero, zero, zero))


def columns(h, width):
    return pl.ds(pl.multiple_of(h * width, width), width)


def wait_for(count, make):
    def body(_, carry):
        make().wait()
        return carry

    lax.fori_loop(0, count, body, 0)


def pack_temporal(kind, win, rows, slots, width):
    chunks = rows[0].shape[0]

    def kernel(kind_ref, win_ref, q_ref, k_ref, v_ref, out_ref, sem):
        def copy(a, ref, h, t):
            quarter = lax.div(t, jnp.int32(slots))
            slot = lax.rem(t, jnp.int32(slots))
            return pltpu.make_async_copy(
                ref.at[:, :, columns(h, width)],
                out_ref.at[pl.ds(quarter * chunks, chunks), a, slot],
                sem,
            )

        def on_temporal(h, t):
            for a, ref in enumerate((q_ref, k_ref, v_ref)):
                copy(a, ref, h, t).start()

        seen, _, _ = head_loop(kind_ref, win_ref, 0, on_temporal, None)
        wait_for(seen * 3, lambda: copy(0, q_ref, jnp.int32(0), jnp.int32(0)))

    return pl.pallas_call(
        kernel,
        out_shape=jax.ShapeDtypeStruct((4 * chunks, 3, slots, TILE, width), BF16),
        in_specs=[SMEM] * 2 + [HBM] * 3,
        out_specs=VMEM,
        scratch_shapes=[pltpu.SemaphoreType.DMA],
        compiler_params=params(8),
        cost_estimate=cost(0, 8 * slots * chunks * 3 * TILE * width * 2),
        name="pack_temporal",
    )(kind, win, *rows)


def pack_spatial(kind, win, w_count, rows, first, slots, width, after=()):
    count = rows[0].shape[0]

    def kernel(kind_ref, win_ref, wide_ref, q_ref, k_ref, v_ref, *rest):
        outs, sem = rest[-5:-1], rest[-1]
        here = chip_here()

        def copy(a, ref, h, slot, out_ref):
            return pltpu.make_async_copy(ref.at[:, columns(h, width)], out_ref.at[slot, a], sem)

        def on_spatial(h, r):
            slot = lax.div(r, jnp.int32(4)) - first
            step = lax.rem(lax.rem(r, jnp.int32(4)) + 4 - here, jnp.int32(4))
            inside = (slot >= 0) & (slot < slots)
            for d in range(4):

                @pl.when(inside & (step == d))
                def _(d=d):
                    for a, ref in enumerate((q_ref, k_ref, v_ref)):
                        copy(a, ref, h, slot, outs[d]).start()

        _, wide, narrow = head_loop(kind_ref, win_ref, wide_ref[0], None, on_spatial)
        held = jnp.clip(wide + narrow - 4 * first, 0, 4 * slots)
        wait_for(held * 3, lambda: copy(0, q_ref, jnp.int32(0), jnp.int32(0), outs[0]))

    return pl.pallas_call(
        kernel,
        out_shape=[jax.ShapeDtypeStruct((slots, 3, count, width), BF16)] * 4,
        in_specs=[SMEM] * 3 + [HBM] * 3 + [ANY] * len(after),
        out_specs=[VMEM] * 4,
        scratch_shapes=[pltpu.SemaphoreType.DMA],
        compiler_params=params(8),
        cost_estimate=cost(0, 4 * slots * 3 * count * width),
        name="pack_spatial",
    )(kind, win, w_count, *rows, *after)


def assemble(blocks, first, slots):
    _, _, rows, width = blocks[0].shape

    def kernel(*refs):
        ins, out, sems = refs[:4], refs[4], refs[5]
        copies = [
            pltpu.make_async_copy(
                ins[d].at[pl.ds(first, slots), pl.ds(1, 2)], out.at[:, :, d], sems.at[d]
            )
            for d in range(4)
        ]
        for c in copies:
            c.start()
        for c in copies:
            c.wait()

    return pl.pallas_call(
        kernel,
        out_shape=jax.ShapeDtypeStruct((slots, 2, 4, rows, width), BF16),
        in_specs=[VMEM] * 4,
        out_specs=VMEM,
        scratch_shapes=[pltpu.SemaphoreType.DMA((4,))],
        compiler_params=params(8),
        cost_estimate=cost(0, 4 * slots * rows * width),
        name="assemble",
    )(*blocks).reshape(slots, 2, 4 * rows, width)


def join(parts, after=()):
    count = parts[0].shape[0]

    def kernel(*refs):
        ins, out, sems = refs[: len(parts)], refs[-2], refs[-1]
        copies = [
            pltpu.make_async_copy(ins[i], out.at[pl.ds(i * count, count)], sems.at[i])
            for i in range(len(parts))
        ]
        for c in copies:
            c.start()
        for c in copies:
            c.wait()

    return pl.pallas_call(
        kernel,
        out_shape=jax.ShapeDtypeStruct((count * len(parts), *parts[0].shape[1:]), BF16),
        in_specs=[VMEM] * len(parts) + [ANY] * len(after),
        out_specs=VMEM,
        scratch_shapes=[pltpu.SemaphoreType.DMA((len(parts),))],
        compiler_params=params(16),
        cost_estimate=cost(0, parts[0].size),
        name="join",
    )(*parts, *after)


def attend(query, pairs, scale, mask=None):
    scores = [
        lax.dot_general(query, key, (((1,), (1,)), ((), ())), preferred_element_type=F32)
        for key, _ in pairs
    ]
    if mask is not None:
        scores = [jnp.where(mask, s, F32(-1e30)) for s in scores]
    tops = [jnp.max(s, axis=1, keepdims=True) for s in scores]
    top = functools.reduce(jnp.maximum, tops)
    total = None
    mixed = None
    for s, (_, value) in zip(scores, pairs):
        weights = jnp.exp2((s - top) * F32(scale * LOG2E))
        part = jnp.sum(weights, axis=1, keepdims=True)
        out = jnp.dot(weights.astype(BF16), value, preferred_element_type=F32)
        total = part if total is None else total + part
        mixed = out if mixed is None else mixed + out
    return (mixed / total).astype(BF16)


def temporal_attention(packed, after=()):
    frames, _, slots, tile, width = packed.shape
    group = 8
    rows = frames * group
    scale = width ** (-0.5)

    def kernel(in_ref, *rest):
        out_ref = rest[-1]
        place_q = lax.broadcasted_iota(jnp.int32, (rows, rows), 0) & (group - 1)
        place_k = lax.broadcasted_iota(jnp.int32, (rows, rows), 1) & (group - 1)
        mask = place_q == place_k
        for j in range(slots):
            arrays = [in_ref[:, a, j] for a in range(3)]
            outs = []
            for g in range(0, tile, group):
                query, key, value = (x[:, g : g + group].reshape(rows, width) for x in arrays)
                out = attend(query, [(key, value)], scale, mask)
                outs.append(out.reshape(frames, group, width))
            out_ref[:, j] = jnp.concatenate(outs, axis=1)

    return pl.pallas_call(
        kernel,
        out_shape=jax.ShapeDtypeStruct((frames, slots, tile, width), BF16),
        in_specs=[VMEM] + [ANY] * len(after),
        out_specs=VMEM,
        compiler_params=params(24),
        cost_estimate=cost(0, slots * rows * width),
        name="temporal_attention",
    )(packed, *after)


def spatial_attention(t_count, w_count, blocks, first, count, kvs, heads, after=()):
    _, _, rows, width = blocks[0].shape
    keys = kvs[0].shape[2]
    scale = width ** (-0.5)
    far = len(kvs) > 2

    def kernel(t_ref, w_ref, *refs):
        queries, kv_refs, outs = refs[:4], refs[4 : 4 + len(kvs)], refs[-4:]
        frame = lax.axis_index("seq")
        rank = (pl.program_id(0) + first) * 4 + chip_here()
        used = rank < heads - t_ref[0]

        def run(chosen):
            pairs = [(kv_refs[i][0, 0], kv_refs[i][0, 1]) for i in chosen]
            for d in range(0, 4, 2):
                query = jnp.concatenate([queries[d][0, 0], queries[d + 1][0, 0]], axis=0)
                out = attend(query, pairs, scale)
                outs[d][0] = out[:rows]
                outs[d + 1][0] = out[rows:]

        if not far:
            pl.when(used)(lambda: run((0, 1)))
        else:
            wide = rank < w_ref[0]
            past = wide & (frame > 0)
            coming = wide & (frame < lax.axis_size("seq") - 1)
            pl.when(used & past & coming)(lambda: run(range(6)))
            pl.when(used & past & jnp.logical_not(coming))(lambda: run(range(4)))
            pl.when(used & coming & jnp.logical_not(past))(lambda: run((0, 1, 4, 5)))
            pl.when(used & jnp.logical_not(past | coming))(lambda: run((0, 1)))

    return pl.pallas_call(
        kernel,
        grid=(count,),
        out_shape=[jax.ShapeDtypeStruct((count, rows, width), BF16)] * 4,
        in_specs=[SMEM] * 2
        + [pl.BlockSpec((1, 1, rows, width), lambda j: (j + first, 0, 0, 0))] * 4
        + [pl.BlockSpec((1, 2, keys, width), lambda j: (j, 0, 0, 0))] * min(5, len(kvs))
        + [pl.BlockSpec((1, 2, keys, width), lambda j: (j + count, 0, 0, 0))] * (len(kvs) // 6)
        + [ANY] * len(after),
        out_specs=[pl.BlockSpec((1, rows, width), lambda j: (j, 0, 0))] * 4,
        compiler_params=params(20),
        cost_estimate=cost(0, count * rows * width),
        name="spatial_attention",
    )(t_count, w_count, *[in_hbm(x) for x in (*blocks, *kvs)], *after)


def unpack(kind, win, w_count, temporal, wide_outs, narrow_outs, heads):
    frames, t_slots, tile, width = temporal.shape
    chunks = frames // 4
    wide_slots = wide_outs[0].shape[0]
    outs = list(wide_outs) + list(narrow_outs)
    groups = len(outs) // 4

    def kernel(kind_ref, win_ref, wide_ref, t_ref, *rest):
        s_refs, out_ref, sem = rest[: 4 * groups], rest[4 * groups], rest[4 * groups + 1]
        here = chip_here()

        def copy(h, src):
            return pltpu.make_async_copy(src, out_ref.at[:, :, columns(h, width)], sem)

        def on_temporal(h, t):
            quarter = lax.div(t, jnp.int32(t_slots))
            slot = lax.rem(t, jnp.int32(t_slots))
            copy(h, t_ref.at[pl.ds(quarter * chunks, chunks), slot]).start()

        def on_spatial(h, r):
            slot = lax.div(r, jnp.int32(4))
            step = lax.rem(lax.rem(r, jnp.int32(4)) + 4 - here, jnp.int32(4))
            for g in range(groups):
                inside = slot < wide_slots if g == 0 else slot >= wide_slots
                if groups == 1:
                    inside = slot >= 0
                for d in range(4):

                    @pl.when(inside & (step == d))
                    def _(g=g, d=d):
                        copy(h, s_refs[4 * g + d].at[slot - g * wide_slots]).start()

        head_loop(kind_ref, win_ref, wide_ref[0], on_temporal, on_spatial)
        wait_for(heads, lambda: copy(jnp.int32(0), t_ref.at[pl.ds(0, chunks), 0]))

    return pl.pallas_call(
        kernel,
        out_shape=pltpu.HBM((chunks, tile, heads * width), BF16),
        in_specs=[SMEM] * 3 + [VMEM] * (1 + 4 * groups),
        out_specs=HBM,
        scratch_shapes=[pltpu.SemaphoreType.DMA],
        compiler_params=params(8),
        cost_estimate=cost(0, 2 * heads * chunks * tile * width * 2),
        name="unpack",
    )(kind, win, w_count, temporal, *[in_hbm(o.reshape(-1, chunks, tile, width)) for o in outs])


def y_step(value, by):
    size = lax.axis_size("head")
    pairs = [(i, (i + 2 * by) % size) for i in range(size)]
    return lax.ppermute(value, "head", pairs)


def sibling(value):
    size = lax.axis_size("head")
    return lax.ppermute(value, "head", [(i, i ^ 1) for i in range(size)])


def next_frame(value, by):
    size = lax.axis_size("seq")
    pairs = [(i, i + by) for i in range(size) if 0 <= i + by < size]
    return lax.ppermute(value, "seq", pairs)


def variant(t_slots, s_slots, wide, query_rows, key_rows, value_rows, kind, win, t_count, w_count):
    heads = kind.shape[0]
    count, total_width = query_rows.shape
    width = total_width // heads
    frames = lax.axis_size("seq")
    rows = (query_rows, key_rows, value_rows)
    tiled = [r.reshape(count // TILE, TILE, total_width) for r in rows]

    packed = pack_temporal(kind, win, tiled, t_slots, width)
    arrived = lax.all_to_all(
        packed.reshape(frames, -1, width), "seq", split_axis=0, concat_axis=0, tiled=True
    ).reshape(packed.shape)

    def exchanged(mine, by=1):
        return [mine[0]] + [y_step(mine[d], by * d) for d in range(1, 4)]

    blocks = exchanged(pack_spatial(kind, win, w_count, rows, 0, s_slots, width))
    kv = assemble(blocks, 0, wide)
    before, after = next_frame(kv, 1), next_frame(kv, -1)
    kv_other = sibling(kv)
    narrow_back = []
    if s_slots > wide:
        kv_n = assemble(blocks, wide, s_slots - wide)
        kvs = [kv_n, sibling(kv_n)]
        narrow = spatial_attention(
            t_count, w_count, blocks, wide, s_slots - wide, kvs, heads, [kv_other]
        )
        narrow_back = exchanged(narrow, -1)
    mixed = temporal_attention(arrived)
    far = sibling(join([before, after], narrow_back[1:]))
    kvs = [kv, kv_other, before, far, after, far]
    wide_outs = spatial_attention(t_count, w_count, blocks, 0, wide, kvs, heads, [mixed])
    wide_back = exchanged(wide_outs, -1)
    returned = lax.all_to_all(
        mixed.reshape(frames, -1, width), "seq", split_axis=0, concat_axis=0, tiled=True
    ).reshape(mixed.shape)
    out = unpack(kind, win, w_count, returned, wide_back, narrow_back, heads)
    return out.reshape(count, total_width)


def on_device(query_rows, key_rows, value_rows, head_kind, frame_window):
    heads = head_kind.shape[0]
    t_count = jnp.sum(head_kind)
    w_count = jnp.sum((1 - head_kind) * frame_window)
    t_need = (t_count + 3) // 4
    s_need = (heads - t_count + 3) // 4
    w_need = (w_count + 3) // 4
    choice = jnp.int32(len(VARIANTS) - 1)
    for i in reversed(range(len(VARIANTS) - 1)):
        t_room, s_room, w_room = VARIANTS[i]
        fits = (t_need <= t_room) & (s_need <= s_room) & (w_need <= w_room)
        choice = jnp.where(fits, jnp.int32(i), choice)
    return lax.switch(
        choice,
        [functools.partial(variant, *v) for v in VARIANTS],
        query_rows,
        key_rows,
        value_rows,
        head_kind,
        frame_window,
        t_count.reshape(1),
        w_count.reshape(1),
    )


def solution(mesh):
    split = P(("seq", "head"), None)
    return jax.shard_map(
        on_device,
        mesh=mesh,
        in_specs=(split, split, split, P(), P()),
        out_specs=split,
        check_vma=False,
    )
```

```python
import functools

import jax
import jax.numpy as jnp
from jax import lax
from jax.experimental import pallas as pl
from jax.experimental.pallas import tpu as pltpu
from jax.sharding import PartitionSpec as P

BF16 = jnp.bfloat16
F32 = jnp.float32
LOG2E = 1.4426950408889634
SMEM = pl.BlockSpec(memory_space=pltpu.SMEM)
HBM = pl.BlockSpec(memory_space=pltpu.HBM)
ANY = pl.BlockSpec(memory_space=pl.ANY)
VMEM = pl.BlockSpec(memory_space=pltpu.VMEM)
MIB = 1024 * 1024
TILE = 16

VARIANTS = (
    (6, 6, 4),
    (10, 10, 10),
)


def in_hbm(value):
    return pltpu.with_memory_space_constraint(value, pltpu.HBM)


def params(vmem=1):
    return pltpu.CompilerParams(vmem_limit_bytes=vmem * MIB)


def cost(flops, bytes_accessed):
    return pl.CostEstimate(flops=flops, bytes_accessed=bytes_accessed, transcendentals=0)


def chip_here():
    return lax.div(lax.axis_index("head"), jnp.int32(2))


def head_loop(kind_ref, win_ref, wide, on_temporal, on_spatial):
    total = kind_ref.shape[0]

    def body(h, counts):
        seen_t, seen_w, seen_n = counts
        is_t = kind_ref[h]
        is_w = (1 - is_t) * win_ref[h]
        is_n = (1 - is_t) * (1 - win_ref[h])
        if on_temporal is not None:
            pl.when(is_t == 1)(lambda: on_temporal(h, seen_t))
        if on_spatial is not None:
            rank = jnp.where(is_w == 1, seen_w, wide + seen_n)
            pl.when(is_t == 0)(lambda: on_spatial(h, rank))
        return seen_t + is_t, seen_w + is_w, seen_n + is_n

    zero = jnp.int32(0)
    return lax.fori_loop(0, total, body, (zero, zero, zero))


def columns(h, width):
    return pl.ds(pl.multiple_of(h * width, width), width)


def wait_for(count, make):
    def body(_, carry):
        make().wait()
        return carry

    lax.fori_loop(0, count, body, 0)


def pack_temporal(kind, win, rows, slots, width):
    chunks = rows[0].shape[0]

    def kernel(kind_ref, win_ref, q_ref, k_ref, v_ref, out_ref, sem):
        def copy(a, ref, h, t):
            quarter = lax.div(t, jnp.int32(slots))
            slot = lax.rem(t, jnp.int32(slots))
            return pltpu.make_async_copy(
                ref.at[:, :, columns(h, width)],
                out_ref.at[pl.ds(quarter * chunks, chunks), a, slot],
                sem,
            )

        def on_temporal(h, t):
            for a, ref in enumerate((q_ref, k_ref, v_ref)):
                copy(a, ref, h, t).start()

        seen, _, _ = head_loop(kind_ref, win_ref, 0, on_temporal, None)
        wait_for(seen * 3, lambda: copy(0, q_ref, jnp.int32(0), jnp.int32(0)))

    return pl.pallas_call(
        kernel,
        out_shape=jax.ShapeDtypeStruct((4 * chunks, 3, slots, TILE, width), BF16),
        in_specs=[SMEM] * 2 + [HBM] * 3,
        out_specs=VMEM,
        scratch_shapes=[pltpu.SemaphoreType.DMA],
        compiler_params=params(8),
        cost_estimate=cost(0, 8 * slots * chunks * 3 * TILE * width * 2),
        name="pack_temporal",
    )(kind, win, *rows)


def pack_spatial(kind, win, w_count, rows, first, slots, width, after=()):
    count = rows[0].shape[0]

    def kernel(kind_ref, win_ref, wide_ref, q_ref, k_ref, v_ref, *rest):
        outs, sem = rest[-5:-1], rest[-1]
        here = chip_here()

        def copy(a, ref, h, slot, out_ref):
            return pltpu.make_async_copy(ref.at[:, columns(h, width)], out_ref.at[slot, a], sem)

        def on_spatial(h, r):
            slot = lax.div(r, jnp.int32(4)) - first
            step = lax.rem(lax.rem(r, jnp.int32(4)) + 4 - here, jnp.int32(4))
            inside = (slot >= 0) & (slot < slots)
            for d in range(4):

                @pl.when(inside & (step == d))
                def _(d=d):
                    for a, ref in enumerate((q_ref, k_ref, v_ref)):
                        copy(a, ref, h, slot, outs[d]).start()

        _, wide, narrow = head_loop(kind_ref, win_ref, wide_ref[0], None, on_spatial)
        held = jnp.clip(wide + narrow - 4 * first, 0, 4 * slots)
        wait_for(held * 3, lambda: copy(0, q_ref, jnp.int32(0), jnp.int32(0), outs[0]))

    return pl.pallas_call(
        kernel,
        out_shape=[jax.ShapeDtypeStruct((slots, 3, count, width), BF16)] * 4,
        in_specs=[SMEM] * 3 + [HBM] * 3 + [ANY] * len(after),
        out_specs=[VMEM] * 4,
        scratch_shapes=[pltpu.SemaphoreType.DMA],
        compiler_params=params(8),
        cost_estimate=cost(0, 4 * slots * 3 * count * width),
        name="pack_spatial",
    )(kind, win, w_count, *rows, *after)


def assemble(blocks, first, slots):
    _, _, rows, width = blocks[0].shape

    def kernel(*refs):
        ins, out, sems = refs[:4], refs[4], refs[5]
        copies = [
            pltpu.make_async_copy(
                ins[d].at[pl.ds(first, slots), pl.ds(1, 2)], out.at[:, :, d], sems.at[d]
            )
            for d in range(4)
        ]
        for c in copies:
            c.start()
        for c in copies:
            c.wait()

    return pl.pallas_call(
        kernel,
        out_shape=jax.ShapeDtypeStruct((slots, 2, 4, rows, width), BF16),
        in_specs=[VMEM] * 4,
        out_specs=VMEM,
        scratch_shapes=[pltpu.SemaphoreType.DMA((4,))],
        compiler_params=params(8),
        cost_estimate=cost(0, 4 * slots * rows * width),
        name="assemble",
    )(*blocks).reshape(slots, 2, 4 * rows, width)


def gate(parts, after):
    count = len(parts)

    def kernel(*refs):
        ins, outs, sems = refs[:count], refs[-count - 1 : -1], refs[-1]
        copies = [pltpu.make_async_copy(ins[i], outs[i], sems.at[i]) for i in range(count)]
        for c in copies:
            c.start()
        for c in copies:
            c.wait()

    return pl.pallas_call(
        kernel,
        out_shape=[jax.ShapeDtypeStruct(p.shape, BF16) for p in parts],
        in_specs=[VMEM] * count + [ANY] * len(after),
        out_specs=[VMEM] * count,
        scratch_shapes=[pltpu.SemaphoreType.DMA((count,))],
        compiler_params=params(16),
        cost_estimate=cost(0, 1024),
        name="gate",
    )(*parts, *after)


def attend(query, pairs, scale, mask=None, counts=None):
    counts = counts or [None] * len(pairs)
    scores = [
        lax.dot_general(query, key, (((1,), (1,)), ((), ())), preferred_element_type=F32)
        for key, _ in pairs
    ]
    if mask is not None:
        scores = [jnp.where(mask, s, F32(-1e30)) for s in scores]
    tops = [jnp.max(s, axis=1, keepdims=True) for s in scores]
    top = functools.reduce(
        jnp.maximum,
        [t if c is None else jnp.where(c, t, F32(-1e30)) for t, c in zip(tops, counts)],
    )
    total = None
    mixed = None
    for s, t, c, (_, value) in zip(scores, tops, counts, pairs):
        weights = jnp.exp2((s - (top if c is None else jnp.maximum(top, t))) * F32(scale * LOG2E))
        part = jnp.sum(weights, axis=1, keepdims=True)
        out = jnp.dot(weights.astype(BF16), value, preferred_element_type=F32)
        if c is not None:
            part, out = jnp.where(c, part, F32(0.0)), jnp.where(c, out, F32(0.0))
        total = part if total is None else total + part
        mixed = out if mixed is None else mixed + out
    return (mixed / total).astype(BF16)


def temporal_attention(packed, after=()):
    frames, _, slots, tile, width = packed.shape
    group = 8
    rows = frames * group
    scale = width ** (-0.5)

    def kernel(in_ref, *rest):
        out_ref = rest[-1]
        place_q = lax.broadcasted_iota(jnp.int32, (rows, rows), 0) & (group - 1)
        place_k = lax.broadcasted_iota(jnp.int32, (rows, rows), 1) & (group - 1)
        mask = place_q == place_k
        def one(j):
            arrays = [in_ref[:, a, j] for a in range(3)]
            outs = []
            for g in range(0, tile, group):
                query, key, value = (x[:, g : g + group].reshape(rows, width) for x in arrays)
                out = attend(query, [(key, value)], scale, mask)
                outs.append(out.reshape(frames, group, width))
            out_ref[:, j] = jnp.concatenate(outs, axis=1)

        if slots < 8:
            for j in range(slots):
                one(j)
        else:
            pl.loop(0, slots)(one)

    return pl.pallas_call(
        kernel,
        out_shape=jax.ShapeDtypeStruct((frames, slots, tile, width), BF16),
        in_specs=[VMEM] + [ANY] * len(after),
        out_specs=VMEM,
        compiler_params=params(24),
        cost_estimate=cost(0, slots * rows * width),
        name="temporal_attention",
    )(packed, *after)


def spatial_attention(t_count, w_count, blocks, first, count, kvs, heads, after=()):
    _, _, rows, width = blocks[0].shape
    keys = kvs[0].shape[2]
    scale = width ** (-0.5)
    far = len(kvs) > 2

    def kernel(t_ref, w_ref, *refs):
        queries, kv_refs, outs = refs[:4], refs[4 : 4 + len(kvs)], refs[-4:]
        frame = lax.axis_index("seq")
        rank = (pl.program_id(0) + first) * 4 + chip_here()
        used = rank < heads - t_ref[0]

        def run(refs, counts):
            pairs = [(r[0, 0], r[0, 1]) for r in refs]
            for d in range(0, 4, 2):
                query = jnp.concatenate([queries[d][0, 0], queries[d + 1][0, 0]], axis=0)
                out = attend(query, pairs, scale, None, counts)
                outs[d][0] = out[:rows]
                outs[d + 1][0] = out[rows:]

        wide = (rank < w_ref[0]) if far else (rank < 0)
        pl.when(used & jnp.logical_not(wide))(lambda: run(kv_refs[:2], None))
        if far:
            past, coming = frame > 0, frame < lax.axis_size("seq") - 1
            counts = [None, None, past, past, coming, coming]
            pl.when(used & wide)(lambda: run(kv_refs, counts))

    return pl.pallas_call(
        kernel,
        grid=(count,),
        out_shape=[jax.ShapeDtypeStruct((count, rows, width), BF16)] * 4,
        in_specs=[SMEM] * 2
        + [pl.BlockSpec((1, 1, rows, width), lambda j: (j + first, 0, 0, 0))] * 4
        + [pl.BlockSpec((1, 2, keys, width), lambda j: (j, 0, 0, 0))] * len(kvs)
        + [ANY] * len(after),
        out_specs=[pl.BlockSpec((1, rows, width), lambda j: (j, 0, 0))] * 4,
        compiler_params=params(20),
        cost_estimate=cost(0, count * rows * width),
        name="spatial_attention",
    )(t_count, w_count, *[in_hbm(x) for x in (*blocks, *kvs)], *after)


def unpack(kind, win, w_count, temporal, wide_outs, narrow_outs, heads):
    frames, t_slots, tile, width = temporal.shape
    chunks = frames // 4
    wide_slots = wide_outs[0].shape[0]
    outs = list(wide_outs) + list(narrow_outs)
    groups = len(outs) // 4

    def kernel(kind_ref, win_ref, wide_ref, t_ref, *rest):
        s_refs, out_ref, sem = rest[: 4 * groups], rest[4 * groups], rest[4 * groups + 1]
        here = chip_here()

        def copy(h, src):
            return pltpu.make_async_copy(src, out_ref.at[:, :, columns(h, width)], sem)

        def on_temporal(h, t):
            quarter = lax.div(t, jnp.int32(t_slots))
            slot = lax.rem(t, jnp.int32(t_slots))
            copy(h, t_ref.at[pl.ds(quarter * chunks, chunks), slot]).start()

        def on_spatial(h, r):
            slot = lax.div(r, jnp.int32(4))
            step = lax.rem(lax.rem(r, jnp.int32(4)) + 4 - here, jnp.int32(4))
            for g in range(groups):
                inside = slot < wide_slots if g == 0 else slot >= wide_slots
                if groups == 1:
                    inside = slot >= 0
                for d in range(4):

                    @pl.when(inside & (step == d))
                    def _(g=g, d=d):
                        copy(h, s_refs[4 * g + d].at[slot - g * wide_slots]).start()

        head_loop(kind_ref, win_ref, wide_ref[0], on_temporal, on_spatial)
        wait_for(heads, lambda: copy(jnp.int32(0), t_ref.at[pl.ds(0, chunks), 0]))

    return pl.pallas_call(
        kernel,
        out_shape=pltpu.HBM((chunks, tile, heads * width), BF16),
        in_specs=[SMEM] * 3 + [VMEM] * (1 + 4 * groups),
        out_specs=HBM,
        scratch_shapes=[pltpu.SemaphoreType.DMA],
        compiler_params=params(8),
        cost_estimate=cost(0, 2 * heads * chunks * tile * width * 2),
        name="unpack",
    )(kind, win, w_count, temporal, *[in_hbm(o.reshape(-1, chunks, tile, width)) for o in outs])


def y_step(value, by):
    size = lax.axis_size("head")
    pairs = [(i, (i + 2 * by) % size) for i in range(size)]
    return lax.ppermute(value, "head", pairs)


def sibling(value):
    size = lax.axis_size("head")
    return lax.ppermute(value, "head", [(i, i ^ 1) for i in range(size)])


def next_frame(value, by):
    size = lax.axis_size("seq")
    pairs = [(i, i + by) for i in range(size) if 0 <= i + by < size]
    return lax.ppermute(value, "seq", pairs)


def variant(t_slots, s_slots, wide, query_rows, key_rows, value_rows, kind, win, t_count, w_count):
    heads = kind.shape[0]
    count, total_width = query_rows.shape
    width = total_width // heads
    frames = lax.axis_size("seq")
    rows = (query_rows, key_rows, value_rows)
    tiled = [r.reshape(count // TILE, TILE, total_width) for r in rows]

    packed = pack_temporal(kind, win, tiled, t_slots, width)
    arrived = lax.all_to_all(
        packed.reshape(frames, -1, width), "seq", split_axis=0, concat_axis=0, tiled=True
    ).reshape(packed.shape)

    def exchanged(mine, by=1):
        return [mine[0]] + [y_step(mine[d], by * d) for d in range(1, 4)]

    blocks = exchanged(pack_spatial(kind, win, w_count, rows, 0, s_slots, width))
    kv = assemble(blocks, 0, wide)
    before, after = next_frame(kv, 1), next_frame(kv, -1)
    kv_other = sibling(kv)
    narrow_back = []
    if s_slots > wide:
        kv_n = assemble(blocks, wide, s_slots - wide)
        kvs = [kv_n, sibling(kv_n)]
        narrow = spatial_attention(
            t_count, w_count, blocks, wide, s_slots - wide, kvs, heads, [kv_other]
        )
        narrow_back = exchanged(narrow, -1)
    mixed = temporal_attention(arrived, narrow_back[1:])
    before_copy, after_copy = gate([before, after], [mixed])
    kvs = [kv, kv_other, before, sibling(before_copy), after, sibling(after_copy)]
    wide_outs = spatial_attention(t_count, w_count, blocks, 0, wide, kvs, heads, [mixed])
    wide_back = exchanged(wide_outs, -1)
    returned = lax.all_to_all(
        mixed.reshape(frames, -1, width), "seq", split_axis=0, concat_axis=0, tiled=True
    ).reshape(mixed.shape)
    out = unpack(kind, win, w_count, returned, wide_back, narrow_back, heads)
    return out.reshape(count, total_width)


def on_device(query_rows, key_rows, value_rows, head_kind, frame_window):
    heads = head_kind.shape[0]
    t_count = jnp.sum(head_kind)
    w_count = jnp.sum((1 - head_kind) * frame_window)
    t_need = (t_count + 3) // 4
    s_need = (heads - t_count + 3) // 4
    w_need = (w_count + 3) // 4
    choice = jnp.int32(len(VARIANTS) - 1)
    for i in reversed(range(len(VARIANTS) - 1)):
        t_room, s_room, w_room = VARIANTS[i]
        fits = (t_need <= t_room) & (s_need <= s_room) & (w_need <= w_room)
        choice = jnp.where(fits, jnp.int32(i), choice)
    return lax.switch(
        choice,
        [functools.partial(variant, *v) for v in VARIANTS],
        query_rows,
        key_rows,
        value_rows,
        head_kind,
        frame_window,
        t_count.reshape(1),
        w_count.reshape(1),
    )


def solution(mesh):
    split = P(("seq", "head"), None)
    return jax.shard_map(
        on_device,
        mesh=mesh,
        in_specs=(split, split, split, P(), P()),
        out_specs=split,
        check_vma=False,
    )
```

```python
import functools

import jax
import jax.numpy as jnp
from jax import lax
from jax.experimental import pallas as pl
from jax.experimental.pallas import tpu as pltpu
from jax.sharding import PartitionSpec as P

BF16 = jnp.bfloat16
F32 = jnp.float32
LOG2E = 1.4426950408889634
SMEM = pl.BlockSpec(memory_space=pltpu.SMEM)
HBM = pl.BlockSpec(memory_space=pltpu.HBM)
ANY = pl.BlockSpec(memory_space=pl.ANY)
VMEM = pl.BlockSpec(memory_space=pltpu.VMEM)
MIB = 1024 * 1024
TILE = 16

VARIANTS = (
    (6, 6, 4),
    (10, 10, 10),
)


def in_hbm(value):
    return pltpu.with_memory_space_constraint(value, pltpu.HBM)


def params(vmem=1):
    return pltpu.CompilerParams(vmem_limit_bytes=vmem * MIB)


def cost(flops, bytes_accessed):
    return pl.CostEstimate(flops=flops, bytes_accessed=bytes_accessed, transcendentals=0)


def chip_here():
    return lax.div(lax.axis_index("head"), jnp.int32(2))


def head_loop(kind_ref, win_ref, wide, on_temporal, on_spatial):
    total = kind_ref.shape[0]

    def body(h, counts):
        seen_t, seen_w, seen_n = counts
        is_t = kind_ref[h]
        is_w = (1 - is_t) * win_ref[h]
        is_n = (1 - is_t) * (1 - win_ref[h])
        if on_temporal is not None:
            pl.when(is_t == 1)(lambda: on_temporal(h, seen_t))
        if on_spatial is not None:
            rank = jnp.where(is_w == 1, seen_w, wide + seen_n)
            pl.when(is_t == 0)(lambda: on_spatial(h, rank))
        return seen_t + is_t, seen_w + is_w, seen_n + is_n

    zero = jnp.int32(0)
    return lax.fori_loop(0, total, body, (zero, zero, zero))


def columns(h, width):
    return pl.ds(pl.multiple_of(h * width, width), width)


def wait_for(count, make):
    def body(_, carry):
        make().wait()
        return carry

    lax.fori_loop(0, count, body, 0)


def pack_temporal(kind, win, rows, slots, width):
    chunks = rows[0].shape[0]

    def kernel(kind_ref, win_ref, q_ref, k_ref, v_ref, out_ref, sem):
        def copy(a, ref, h, t):
            quarter = lax.div(t, jnp.int32(slots))
            slot = lax.rem(t, jnp.int32(slots))
            return pltpu.make_async_copy(
                ref.at[:, :, columns(h, width)],
                out_ref.at[pl.ds(quarter * chunks, chunks), a, slot],
                sem,
            )

        def on_temporal(h, t):
            for a, ref in enumerate((q_ref, k_ref, v_ref)):
                copy(a, ref, h, t).start()

        seen, _, _ = head_loop(kind_ref, win_ref, 0, on_temporal, None)
        wait_for(seen * 3, lambda: copy(0, q_ref, jnp.int32(0), jnp.int32(0)))

    return pl.pallas_call(
        kernel,
        out_shape=jax.ShapeDtypeStruct((4 * chunks, 3, slots, TILE, width), BF16),
        in_specs=[SMEM] * 2 + [HBM] * 3,
        out_specs=VMEM,
        scratch_shapes=[pltpu.SemaphoreType.DMA],
        compiler_params=params(8),
        cost_estimate=cost(0, 8 * slots * chunks * 3 * TILE * width * 2),
        name="pack_temporal",
    )(kind, win, *rows)


def pack_spatial(kind, win, w_count, rows, first, slots, width, after=()):
    count = rows[0].shape[0]

    def kernel(kind_ref, win_ref, wide_ref, q_ref, k_ref, v_ref, *rest):
        outs, sem = rest[-5:-1], rest[-1]
        here = chip_here()

        def copy(a, ref, h, slot, out_ref):
            return pltpu.make_async_copy(ref.at[:, columns(h, width)], out_ref.at[slot, a], sem)

        def on_spatial(h, r):
            slot = lax.div(r, jnp.int32(4)) - first
            step = lax.rem(lax.rem(r, jnp.int32(4)) + 4 - here, jnp.int32(4))
            inside = (slot >= 0) & (slot < slots)
            for d in range(4):

                @pl.when(inside & (step == d))
                def _(d=d):
                    for a, ref in enumerate((q_ref, k_ref, v_ref)):
                        copy(a, ref, h, slot, outs[d]).start()

        _, wide, narrow = head_loop(kind_ref, win_ref, wide_ref[0], None, on_spatial)
        held = jnp.clip(wide + narrow - 4 * first, 0, 4 * slots)
        wait_for(held * 3, lambda: copy(0, q_ref, jnp.int32(0), jnp.int32(0), outs[0]))

    return pl.pallas_call(
        kernel,
        out_shape=[jax.ShapeDtypeStruct((slots, 3, count, width), BF16)] * 4,
        in_specs=[SMEM] * 3 + [HBM] * 3 + [ANY] * len(after),
        out_specs=[VMEM] * 4,
        scratch_shapes=[pltpu.SemaphoreType.DMA],
        compiler_params=params(8),
        cost_estimate=cost(0, 4 * slots * 3 * count * width),
        name="pack_spatial",
    )(kind, win, w_count, *rows, *after)


def assemble(blocks, first, slots):
    _, _, rows, width = blocks[0].shape

    def kernel(*refs):
        ins, out, sems = refs[:4], refs[4], refs[5]
        copies = [
            pltpu.make_async_copy(
                ins[d].at[pl.ds(first, slots), pl.ds(1, 2)], out.at[:, :, d], sems.at[d]
            )
            for d in range(4)
        ]
        for c in copies:
            c.start()
        for c in copies:
            c.wait()

    return pl.pallas_call(
        kernel,
        out_shape=jax.ShapeDtypeStruct((slots, 2, 4, rows, width), BF16),
        in_specs=[VMEM] * 4,
        out_specs=VMEM,
        scratch_shapes=[pltpu.SemaphoreType.DMA((4,))],
        compiler_params=params(8),
        cost_estimate=cost(0, 4 * slots * rows * width),
        name="assemble",
    )(*blocks).reshape(slots, 2, 4 * rows, width)


def gate(parts, after):
    count = len(parts)

    def kernel(*refs):
        del refs

    return pl.pallas_call(
        kernel,
        out_shape=[jax.ShapeDtypeStruct(p.shape, BF16) for p in parts],
        in_specs=[ANY] * (count + len(after)),
        out_specs=[ANY] * count,
        input_output_aliases={i: i for i in range(count)},
        compiler_params=params(),
        cost_estimate=cost(0, 1024),
        name="gate",
    )(*parts, *after)


def attend(query, pairs, scale, mask=None, counts=None):
    counts = counts or [None] * len(pairs)
    scores = [
        lax.dot_general(query, key, (((1,), (1,)), ((), ())), preferred_element_type=F32)
        for key, _ in pairs
    ]
    if mask is not None:
        scores = [jnp.where(mask, s, F32(-1e30)) for s in scores]
    tops = [jnp.max(s, axis=1, keepdims=True) for s in scores]
    top = functools.reduce(
        jnp.maximum,
        [t if c is None else jnp.where(c, t, F32(-1e30)) for t, c in zip(tops, counts)],
    )
    total = None
    mixed = None
    for s, t, c, (_, value) in zip(scores, tops, counts, pairs):
        weights = jnp.exp2((s - (top if c is None else jnp.maximum(top, t))) * F32(scale * LOG2E))
        part = jnp.sum(weights, axis=1, keepdims=True)
        out = jnp.dot(weights.astype(BF16), value, preferred_element_type=F32)
        if c is not None:
            part, out = jnp.where(c, part, F32(0.0)), jnp.where(c, out, F32(0.0))
        total = part if total is None else total + part
        mixed = out if mixed is None else mixed + out
    return (mixed / total).astype(BF16)


def temporal_attention(packed, after=()):
    frames, _, slots, tile, width = packed.shape
    group = 8
    rows = frames * group
    scale = width ** (-0.5)

    def kernel(in_ref, *rest):
        out_ref = rest[-1]
        place_q = lax.broadcasted_iota(jnp.int32, (rows, rows), 0) & (group - 1)
        place_k = lax.broadcasted_iota(jnp.int32, (rows, rows), 1) & (group - 1)
        mask = place_q == place_k
        def one(j):
            arrays = [in_ref[:, a, j] for a in range(3)]
            outs = []
            for g in range(0, tile, group):
                query, key, value = (x[:, g : g + group].reshape(rows, width) for x in arrays)
                out = attend(query, [(key, value)], scale, mask)
                outs.append(out.reshape(frames, group, width))
            out_ref[:, j] = jnp.concatenate(outs, axis=1)

        if slots < 8:
            for j in range(slots):
                one(j)
        else:
            pl.loop(0, slots)(one)

    return pl.pallas_call(
        kernel,
        out_shape=jax.ShapeDtypeStruct((frames, slots, tile, width), BF16),
        in_specs=[VMEM] + [ANY] * len(after),
        out_specs=VMEM,
        compiler_params=params(24),
        cost_estimate=cost(0, slots * rows * width),
        name="temporal_attention",
    )(packed, *after)


def spatial_attention(t_count, w_count, blocks, first, count, kvs, heads, after=()):
    _, _, rows, width = blocks[0].shape
    keys = kvs[0].shape[2]
    scale = width ** (-0.5)
    far = len(kvs) > 2

    def kernel(t_ref, w_ref, *refs):
        queries, kv_refs, outs = refs[:4], refs[4 : 4 + len(kvs)], refs[-4:]
        frame = lax.axis_index("seq")
        rank = (pl.program_id(0) + first) * 4 + chip_here()
        used = rank < heads - t_ref[0]

        def run(refs, counts):
            pairs = [(r[0, 0], r[0, 1]) for r in refs]
            for d in range(0, 4, 2):
                query = jnp.concatenate([queries[d][0, 0], queries[d + 1][0, 0]], axis=0)
                out = attend(query, pairs, scale, None, counts)
                outs[d][0] = out[:rows]
                outs[d + 1][0] = out[rows:]

        wide = (rank < w_ref[0]) if far else (rank < 0)
        pl.when(used & jnp.logical_not(wide))(lambda: run(kv_refs[:2], None))
        if far:
            past, coming = frame > 0, frame < lax.axis_size("seq") - 1
            counts = [None, None, past, past, coming, coming]
            pl.when(used & wide)(lambda: run(kv_refs, counts))

    return pl.pallas_call(
        kernel,
        grid=(count,),
        out_shape=[jax.ShapeDtypeStruct((count, rows, width), BF16)] * 4,
        in_specs=[SMEM] * 2
        + [pl.BlockSpec((1, 1, rows, width), lambda j: (j + first, 0, 0, 0))] * 4
        + [pl.BlockSpec((1, 2, keys, width), lambda j: (j, 0, 0, 0))] * len(kvs)
        + [ANY] * len(after),
        out_specs=[pl.BlockSpec((1, rows, width), lambda j: (j, 0, 0))] * 4,
        compiler_params=params(20),
        cost_estimate=cost(0, count * rows * width),
        name="spatial_attention",
    )(t_count, w_count, *[in_hbm(x) for x in (*blocks, *kvs[:2])], *kvs[2:], *after)


def unpack(kind, win, w_count, temporal, wide_outs, narrow_outs, heads):
    frames, t_slots, tile, width = temporal.shape
    chunks = frames // 4
    wide_slots = wide_outs[0].shape[0]
    outs = list(wide_outs) + list(narrow_outs)
    groups = len(outs) // 4

    def kernel(kind_ref, win_ref, wide_ref, t_ref, *rest):
        s_refs, out_ref, sem = rest[: 4 * groups], rest[4 * groups], rest[4 * groups + 1]
        here = chip_here()

        def copy(h, src):
            return pltpu.make_async_copy(src, out_ref.at[:, :, columns(h, width)], sem)

        def on_temporal(h, t):
            quarter = lax.div(t, jnp.int32(t_slots))
            slot = lax.rem(t, jnp.int32(t_slots))
            copy(h, t_ref.at[pl.ds(quarter * chunks, chunks), slot]).start()

        def on_spatial(h, r):
            slot = lax.div(r, jnp.int32(4))
            step = lax.rem(lax.rem(r, jnp.int32(4)) + 4 - here, jnp.int32(4))
            for g in range(groups):
                inside = slot < wide_slots if g == 0 else slot >= wide_slots
                if groups == 1:
                    inside = slot >= 0
                for d in range(4):

                    @pl.when(inside & (step == d))
                    def _(g=g, d=d):
                        copy(h, s_refs[4 * g + d].at[slot - g * wide_slots]).start()

        head_loop(kind_ref, win_ref, wide_ref[0], on_temporal, on_spatial)
        wait_for(heads, lambda: copy(jnp.int32(0), t_ref.at[pl.ds(0, chunks), 0]))

    return pl.pallas_call(
        kernel,
        out_shape=pltpu.HBM((chunks, tile, heads * width), BF16),
        in_specs=[SMEM] * 3 + [VMEM] * (1 + 4 * groups),
        out_specs=HBM,
        scratch_shapes=[pltpu.SemaphoreType.DMA],
        compiler_params=params(8),
        cost_estimate=cost(0, 2 * heads * chunks * tile * width * 2),
        name="unpack",
    )(kind, win, w_count, temporal, *[in_hbm(o.reshape(-1, chunks, tile, width)) for o in outs])


def y_step(value, by):
    size = lax.axis_size("head")
    pairs = [(i, (i + 2 * by) % size) for i in range(size)]
    return lax.ppermute(value, "head", pairs)


def sibling(value):
    size = lax.axis_size("head")
    return lax.ppermute(value, "head", [(i, i ^ 1) for i in range(size)])


def next_frame(value, by):
    size = lax.axis_size("seq")
    pairs = [(i, i + by) for i in range(size) if 0 <= i + by < size]
    return lax.ppermute(value, "seq", pairs)


def variant(t_slots, s_slots, wide, query_rows, key_rows, value_rows, kind, win, t_count, w_count):
    heads = kind.shape[0]
    count, total_width = query_rows.shape
    width = total_width // heads
    frames = lax.axis_size("seq")
    rows = (query_rows, key_rows, value_rows)
    tiled = [r.reshape(count // TILE, TILE, total_width) for r in rows]

    packed = pack_temporal(kind, win, tiled, t_slots, width)
    arrived = lax.all_to_all(
        packed.reshape(frames, -1, width), "seq", split_axis=0, concat_axis=0, tiled=True
    ).reshape(packed.shape)

    def exchanged(mine, by=1):
        return [mine[0]] + [y_step(mine[d], by * d) for d in range(1, 4)]

    blocks = exchanged(pack_spatial(kind, win, w_count, rows, 0, s_slots, width))
    kv = assemble(blocks, 0, wide)
    before, after = next_frame(kv, 1), next_frame(kv, -1)
    kv_other = sibling(kv)
    narrow_back = []
    if s_slots > wide:
        kv_n = assemble(blocks, wide, s_slots - wide)
        kvs = [kv_n, sibling(kv_n)]
        narrow = spatial_attention(
            t_count, w_count, blocks, wide, s_slots - wide, kvs, heads, [kv_other]
        )
        narrow_back = exchanged(narrow, -1)
    mixed = temporal_attention(arrived, narrow_back[1:])
    before, after = gate([before, after], [mixed])
    kvs = [kv, kv_other, before, sibling(before), after, sibling(after)]
    wide_outs = spatial_attention(t_count, w_count, blocks, 0, wide, kvs, heads, [mixed])
    wide_back = exchanged(wide_outs, -1)
    returned = lax.all_to_all(
        mixed.reshape(frames, -1, width), "seq", split_axis=0, concat_axis=0, tiled=True
    ).reshape(mixed.shape)
    out = unpack(kind, win, w_count, returned, wide_back, narrow_back, heads)
    return out.reshape(count, total_width)


def on_device(query_rows, key_rows, value_rows, head_kind, frame_window):
    heads = head_kind.shape[0]
    t_count = jnp.sum(head_kind)
    w_count = jnp.sum((1 - head_kind) * frame_window)
    t_need = (t_count + 3) // 4
    s_need = (heads - t_count + 3) // 4
    w_need = (w_count + 3) // 4
    choice = jnp.int32(len(VARIANTS) - 1)
    for i in reversed(range(len(VARIANTS) - 1)):
        t_room, s_room, w_room = VARIANTS[i]
        fits = (t_need <= t_room) & (s_need <= s_room) & (w_need <= w_room)
        choice = jnp.where(fits, jnp.int32(i), choice)
    return lax.switch(
        choice,
        [functools.partial(variant, *v) for v in VARIANTS],
        query_rows,
        key_rows,
        value_rows,
        head_kind,
        frame_window,
        t_count.reshape(1),
        w_count.reshape(1),
    )


def solution(mesh):
    split = P(("seq", "head"), None)
    return jax.shard_map(
        on_device,
        mesh=mesh,
        in_specs=(split, split, split, P(), P()),
        out_specs=split,
        check_vma=False,
    )
```
